512 devices in a mesh: dp: 32 (over x, z), sx: 4 (over y_lo), sy: 4 (over y_hi, core).
Axes of the slice: x: 4, y: 8 (y_hi: 2, y_lo: 4; y = y_hi * 4 + y_lo), z: 8, core: 2. Of those that a mesh axis runs over, the one named last changes fastest.
Arguments:
- cotangent: bfloat16 [32, 48, 48, 48, 128], P('dp', 'sx', 'sy'), may hold values from -6 to 6
- spectrum: bfloat16 [2, 32, 8, 8, 4, 128], P(None, 'dp', 'sx', 'sy'), may hold values from -6 to 6
- master: float32 [128, 2, 8, 8, 4, 128], P('dp', None, 'sx', 'sy'), may hold values from -4 to 4
- moment1: float32 [128, 2, 8, 8, 4, 128], P('dp', None, 'sx', 'sy'), may hold values from -24 to 24
- moment2: float32 [128, 2, 8, 8, 4, 128], P('dp', None, 'sx', 'sy'), may hold values from 4 to 256
Outputs:
- input_grad: bfloat16 [32, 48, 48, 48, 128], P('dp', 'sx', 'sy')
- new_master: float32 [128, 2, 8, 8, 4, 128], P('dp', None, 'sx', 'sy')
- new_moment1: float32 [128, 2, 8, 8, 4, 128], P('dp', None, 'sx', 'sy')
- new_moment2: float32 [128, 2, 8, 8, 4, 128], P('dp', None, 'sx', 'sy')
The draws below stay inside these ranges and needn't reach their ends.
All inputs are finite; a program needn't handle non-finite values.
Results may differ from the reference program's by a relative error of at most 0.0067.
Values may be sent and summed in bfloat16 or wider, within the bound.
No kernel may reach another device: no remote copies, remote signals or barrier semaphores. Data moves between devices by JAX's collectives and lax.ppermute only.
A program may use at most 64 MiB of HBM per device.

```python
import math
import jax
import jax.numpy as jnp
from jax import lax

NX = 48
NY = 48
NZ = 48
MX = 8
MY = 8
MZ = 4
CI = 128
CO = 128
STEP = 100
BATCH = 32


def spiked(drawn, own_key, source, target, blocks, factor):
    def block_of(position):
        return (jnp.arange(drawn.shape[position]) // (drawn.shape[position] // blocks)).reshape((-1,) + (1,) * (drawn.ndim - 1 - position))

    near = jax.random.permutation(own_key, blocks)[block_of(target)]
    other_side = (block_of(target) + blocks // 2) % blocks
    return jnp.where((block_of(source) == near) | (block_of(source) == other_side), factor * drawn, drawn)


def block_levels(rng, shape, pieces, low, high):
    loudness = 1.0
    for axis_at, blocks in pieces:
        steps = jax.random.uniform(jax.random.fold_in(jax.random.fold_in(rng, 6), axis_at), (blocks,), jnp.float32, low / len(pieces), high / len(pieces))
        loudness = loudness * jnp.repeat(jnp.exp(steps), shape[axis_at] // blocks).reshape((-1,) + (1,) * (len(shape) - 1 - axis_at))
    return loudness


def scatter_about(key, extent, spread, bound, cuts=(), kind=jnp.bfloat16):
    entries = jax.random.normal(key, extent, jnp.float32) * spread
    if len(cuts) > 0:
        entries = block_levels(key, extent, cuts, -0.22, 0.18) * entries
    return jnp.clip(entries, min=-bound, max=bound).astype(kind)


def heavy_noise(stream_key, extent, spread, limit, pieces, heavy, kind=jnp.bfloat16):
    values = spread * jax.random.normal(stream_key, extent, jnp.float32)
    if pieces:
        values = values * block_levels(stream_key, extent, pieces, -0.22, 0.18)
    return jnp.clip(spiked(values, jax.random.fold_in(stream_key, 3), *heavy), -limit, limit).astype(kind)


def setup_inputs(seed: int = 0) -> dict:
    keys = jax.random.split(jax.random.key(seed), 6)
    return {
        "cotangent": scatter_about(keys[0], (BATCH, NX, NY, NZ, CO), 1.0, 6.0, ((0, 32), (1, 4), (2, 4))),
        "spectrum": heavy_noise(keys[1], (2, BATCH, MX, MY, MZ, CI), 1.0, 6.0, ((1, 32), (2, 4), (3, 4)), (1, 5, 32, 2.75)),
        "master": scatter_about(keys[2], (CI, 2, MX, MY, MZ, CO), 1.0, 4.0, ((0, 32), (2, 4), (3, 4)), jnp.float32),
        "moment1": scatter_about(keys[3], (CI, 2, MX, MY, MZ, CO), 4.0, 24.0, ((0, 32), (2, 4), (3, 4)), jnp.float32),
        "moment2": jnp.clip(jnp.exp(math.log(256.0) - 4.158883 * jax.random.uniform(keys[4], (CI, 2, MX, MY, MZ, CO), jnp.float32) ** block_levels(keys[4], (CI, 2, MX, MY, MZ, CO), ((0, 32), (2, 4), (3, 4)), -0.2, 0.2)), 4.0, 256.0),
    }


exact = lax.Precision.HIGHEST
beta_one = 0.9
beta_two = 0.95
learn_rate = 0.001
epsilon = 1e-08

def mode_numbers(index, count):
    return jnp.where(index < count // 2, index, index - count).astype(jnp.int32)

def phase_tables(places, freqs, length):
    product = places.astype(jnp.int32)[:, None] * freqs.astype(jnp.int32)[..., None, :] % length
    angle = product.astype(jnp.float32) * (2.0 * math.pi / length)
    return (jnp.cos(angle), jnp.sin(angle))

def analyse(parts, cos_table, sin_table, form):
    real_part = jnp.einsum(form, parts[0], cos_table, precision=exact) + jnp.einsum(form, parts[1], sin_table, precision=exact)
    imag_part = jnp.einsum(form, parts[1], cos_table, precision=exact) - jnp.einsum(form, parts[0], sin_table, precision=exact)
    return (real_part, imag_part)

def synthesise(parts, cos_table, sin_table, form):
    real_part = jnp.einsum(form, parts[0], cos_table, precision=exact) - jnp.einsum(form, parts[1], sin_table, precision=exact)
    imag_part = jnp.einsum(form, parts[0], sin_table, precision=exact) + jnp.einsum(form, parts[1], cos_table, precision=exact)
    return (real_part, imag_part)

def reference(cotangent, spectrum, master, moment1, moment2):
    norm = 1.0 / math.sqrt(NX * NY * NZ)
    x_freq = mode_numbers(jnp.arange(MX, dtype=jnp.int32), MX)
    y_freq = mode_numbers(jnp.arange(MY, dtype=jnp.int32), MY)
    z_freq = jnp.arange(MZ, dtype=jnp.int32)
    x_cos, x_sin = phase_tables(jnp.arange(NX, dtype=jnp.int32), x_freq, NX)
    y_cos, y_sin = phase_tables(jnp.arange(NY, dtype=jnp.int32), y_freq, NY)
    z_cos, z_sin = phase_tables(jnp.arange(NZ, dtype=jnp.int32), z_freq, NZ)
    z_narrow = lax.optimization_barrier(jnp.concatenate([z_cos, -z_sin], axis=1).astype(jnp.bfloat16))
    z_table = z_narrow.astype(jnp.float32)
    scale = jnp.where(z_freq > 0, 2.0, 1.0).astype(jnp.float32) * norm

    def analyse_one(snapshot):
        z_part = jnp.einsum('xyzo,zq->xyqo', snapshot.astype(jnp.float32), z_table, precision=exact)
        parts = (z_part[:, :, :MZ], z_part[:, :, MZ:])
        parts = analyse(parts, y_cos, y_sin, 'xylo,ym->xmlo')
        parts = analyse(parts, x_cos, x_sin, 'xmlo,xj->jmlo')
        return jnp.stack([parts[0] * scale[:, None], parts[1] * scale[:, None]]).astype(jnp.bfloat16)
    spectral_cot = jnp.moveaxis(lax.map(analyse_one, cotangent), 0, 1)
    cot_real = spectral_cot[0].astype(jnp.float32)
    cot_imag = spectral_cot[1].astype(jnp.float32)
    input_real = spectrum[0].astype(jnp.float32)
    input_imag = spectrum[1].astype(jnp.float32)
    weight_narrow = lax.optimization_barrier(master.astype(jnp.bfloat16))
    weight_real = weight_narrow[:, 0].astype(jnp.float32)
    weight_imag = weight_narrow[:, 1].astype(jnp.float32)
    form = 'bjmli,bjmlo->ijmlo'
    grad_real = jnp.einsum(form, input_real, cot_real, precision=exact) + jnp.einsum(form, input_imag, cot_imag, precision=exact)
    grad_imag = jnp.einsum(form, input_real, cot_imag, precision=exact) - jnp.einsum(form, input_imag, cot_real, precision=exact)
    weight_grad = jnp.stack([grad_real, grad_imag], axis=1)
    form = 'bjmlo,ijmlo->bjmli'
    mode_real = jnp.einsum(form, cot_real, weight_real, precision=exact) + jnp.einsum(form, cot_imag, weight_imag, precision=exact)
    mode_imag = jnp.einsum(form, cot_imag, weight_real, precision=exact) - jnp.einsum(form, cot_real, weight_imag, precision=exact)
    mode_grad = jnp.stack([mode_real, mode_imag]).astype(jnp.bfloat16)

    def synth_one(modes):
        parts = (modes[0].astype(jnp.float32), modes[1].astype(jnp.float32))
        parts = synthesise(parts, x_cos, x_sin, 'jmli,xj->xmli')
        parts = synthesise(parts, y_cos, y_sin, 'xmli,ym->xyli')
        grid = jnp.einsum('xyli,zl->xyzi', parts[0], z_cos, precision=exact) - jnp.einsum('xyli,zl->xyzi', parts[1], z_sin, precision=exact)
        return (grid * norm).astype(jnp.bfloat16)
    input_grad = lax.map(synth_one, jnp.moveaxis(mode_grad, 1, 0))
    new_moment1 = beta_one * moment1 + (1.0 - beta_one) * weight_grad
    new_moment2 = beta_two * moment2 + (1.0 - beta_two) * weight_grad * weight_grad
    first_fix = 1.0 - beta_one ** STEP
    second_fix = 1.0 - beta_two ** STEP
    new_master = master - learn_rate * (new_moment1 / first_fix) / (jnp.sqrt(new_moment2 / second_fix) + epsilon)
    return (input_grad, new_master, new_moment1, new_moment2)
```

```python
import math

import jax
import jax.numpy as jnp
import ml_dtypes
import numpy as np
from jax import lax
from jax.experimental import pallas as pl
from jax.experimental.pallas import tpu as pltpu
from jax.sharding import PartitionSpec as P

NX = 48
NY = 48
NZ = 48
MX = 8
MY = 8
MZ = 4
CI = 128
CO = 128
STEP = 100

beta_one = 0.9
beta_two = 0.95
learn_rate = 0.001
epsilon = 1e-08
norm = 1.0 / math.sqrt(NX * NY * NZ)

LX = 12
LY = 12
CELLS = LY * NZ
ROWS = MY * MZ
MODES = 16
GROUP = 16
SNAPS = 32
OWN = 4
X_STEP = 4

bf16 = jnp.bfloat16
f32 = jnp.float32


def freqs(count):
    index = np.arange(count)
    return np.where(index < count // 2, index, index - count)


def angles(places, numbers, length):
    return 2.0 * np.pi * ((places[:, None] * numbers[None, :]) % length) / length


def narrow(table):
    return table.astype(np.float32).astype(ml_dtypes.bfloat16)


def high_low(table):
    high = narrow(table)
    return high, narrow(table - high.astype(np.float64))


def x_phases():
    theta = angles(np.arange(NX), np.arange(1, 5), NX)
    return np.stack([np.cos(theta), np.sin(theta)], axis=-1).astype(np.float32).reshape(-1)


def analyse_tables():
    z_angle = angles(np.arange(NZ), np.arange(MZ), NZ)
    z_cos = narrow(np.cos(z_angle)).astype(np.float64)
    z_sin = narrow(-np.sin(z_angle)).astype(np.float64)
    y_angle = angles(np.arange(NY), freqs(MY), NY).reshape(4, LY, MY)
    y_cos, y_sin = np.cos(y_angle), np.sin(y_angle)
    real = np.einsum("dym,zl->dmlyz", y_cos, z_cos) + np.einsum("dym,zl->dmlyz", y_sin, z_sin)
    imag = np.einsum("dym,zl->dmlyz", y_cos, z_sin) - np.einsum("dym,zl->dmlyz", y_sin, z_cos)
    table = np.stack([real, imag], axis=1).reshape(4, 2 * ROWS, CELLS)
    return np.concatenate(high_low(table), axis=1)


def synthesise_tables():
    z_angle = angles(np.arange(NZ), np.arange(MZ), NZ)
    y_angle = angles(np.arange(NY), freqs(MY), NY).reshape(4, LY, MY)
    theta = y_angle[:, :, None, :, None] + z_angle[None, None, :, None, :]
    table = norm * np.stack([np.cos(theta), -np.sin(theta)], axis=3)
    high, low = high_low(table.reshape(4, CELLS, 2 * ROWS))
    return np.concatenate([high, low, high], axis=2)


def analyse_kernel(place, cot, table, phase, out, total):
    step = pl.program_id(0)
    tab = table[0]
    real, imag = [], []
    for j in range(0, X_STEP, 2):
        pair = jnp.concatenate([cot[j], cot[j + 1]], axis=1)
        both = jnp.dot(tab, pair, preferred_element_type=f32)
        part = both[: 2 * ROWS] + both[2 * ROWS :]
        for lanes in (slice(0, CO), slice(CO, 2 * CO)):
            real.append(part[:ROWS, lanes])
            imag.append(part[ROWS:, lanes])
    base = (place[0] * LX + step * X_STEP) * 8

    @pl.when(step == 0)
    def _():
        total[...] = jnp.zeros_like(total)

    total[0, 0] += sum(real)
    total[0, 1] += sum(imag)
    for f in range(1, 5):
        rc = rs = ic = is_ = 0.0
        for j in range(X_STEP):
            cos = phase[base + 8 * j + 2 * f - 2]
            sin = phase[base + 8 * j + 2 * f - 1]
            rc += real[j] * cos
            rs += real[j] * sin
            ic += imag[j] * cos
            is_ += imag[j] * sin
        if f < 4:
            total[f, 0] += rc + is_
            total[f, 1] += ic - rs
        total[MX - f, 0] += rc - is_
        total[MX - f, 1] += ic + rs

    @pl.when(step == LX // X_STEP - 1)
    def _():
        for s in range(GROUP):
            x, y = divmod(s, 4)
            for c in range(2):
                block = [total[2 * x + j, c, 8 * y : 8 * y + 8, :] for j in range(2)]
                out[s, :, c * CO : (c + 1) * CO] = jnp.concatenate(block, axis=0).astype(bf16)


def analyse(place, cotangent):
    return pl.pallas_call(
        analyse_kernel,
        out_shape=jax.ShapeDtypeStruct((GROUP, MODES, 2 * CO), bf16),
        grid_spec=pltpu.PrefetchScalarGridSpec(
            num_scalar_prefetch=1,
            grid=(LX // X_STEP,),
            in_specs=[
                pl.BlockSpec((X_STEP, CELLS, CO), lambda i, p: (i, 0, 0)),
                pl.BlockSpec((1, 4 * ROWS, CELLS), lambda i, p: (p[1], 0, 0)),
                pl.BlockSpec(memory_space=pltpu.SMEM),
            ],
            out_specs=pl.BlockSpec((GROUP, MODES, 2 * CO), lambda i, p: (0, 0, 0)),
            scratch_shapes=[pltpu.VMEM((MX, 2, ROWS, CO), f32)],
        ),
        compiler_params=pltpu.CompilerParams(vmem_limit_bytes=24 * 2**20),
        name="analyse",
    )(place, cotangent, jnp.asarray(analyse_tables()), jnp.asarray(x_phases()))


def own_mode(rows, cols):
    row = lax.broadcasted_iota(jnp.int32, (rows, cols), 0) % MODES
    return row == lax.broadcasted_iota(jnp.int32, (rows, cols), 1) % MODES


def channel_of(rows):
    row = lax.broadcasted_iota(jnp.int32, (rows, CI), 0)
    chan = lax.broadcasted_iota(jnp.int32, (rows, CI), 1)
    return jnp.where(chan == (row % SNAPS) * OWN + row // SNAPS, 1.0, 0.0).astype(bf16)


def mix_kernel(cot, master, spec, out):
    rows, cols = SNAPS * MODES, 2 * OWN * MODES
    weight = master[...].reshape(OWN, 2, MODES, CO)
    real, imag = weight[:, 0], weight[:, 1]
    table = jnp.concatenate(
        [
            jnp.stack([real, -imag], axis=1).reshape(cols, CO),
            jnp.stack([imag, real], axis=1).reshape(cols, CO),
        ],
        axis=1,
    ).astype(bf16)
    every = lax.dot_general(
        cot[...].reshape(rows, 2 * CO), table, (((1,), (1,)), ((), ())), preferred_element_type=f32
    )
    grad = jnp.where(own_mode(rows, cols), every, 0.0).reshape(SNAPS, MODES, cols).sum(axis=1)
    turned = lax.dot_general(
        channel_of(OWN * SNAPS), spec[...], (((1,), (1,)), ((), ())), preferred_element_type=f32
    )
    pieces = [turned[i * SNAPS : (i + 1) * SNAPS] for i in range(OWN)]
    out[...] = jnp.concatenate([grad, *pieces], axis=1).astype(bf16)


def mix(cot, master, spec):
    return pl.pallas_call(
        mix_kernel,
        out_shape=jax.ShapeDtypeStruct((SNAPS, 4 * OWN * MODES), bf16),
        in_specs=[pl.BlockSpec(memory_space=pltpu.VMEM)] * 3,
        out_specs=pl.BlockSpec(memory_space=pltpu.VMEM),
        compiler_params=pltpu.CompilerParams(vmem_limit_bytes=24 * 2**20),
        name="mix",
    )(cot, master, spec)


def turn_kernel(got, out):
    width = 2 * MODES
    grad = got[...][:, : OWN * width]
    stacked = jnp.concatenate([grad[:, i * width : (i + 1) * width] for i in range(OWN)], axis=0)
    turned = lax.dot_general(
        stacked, channel_of(OWN * SNAPS), (((0,), (0,)), ((), ())), preferred_element_type=f32
    )
    out[...] = jnp.broadcast_to(turned.astype(bf16)[None], out.shape)


def turn(got):
    return pl.pallas_call(
        turn_kernel,
        out_shape=jax.ShapeDtypeStruct((GROUP, 2 * MODES, CI), bf16),
        in_specs=[pl.BlockSpec(memory_space=pltpu.VMEM)],
        out_specs=pl.BlockSpec(memory_space=pltpu.VMEM),
        compiler_params=pltpu.CompilerParams(vmem_limit_bytes=24 * 2**20),
        name="turn",
    )(got)


def synthesise_kernel(place, modes, table, phase, out, plus, less):
    step = pl.program_id(0)

    @pl.when(step == 0)
    def _():
        parts = [modes[s].astype(f32) for s in range(GROUP)]

        def field(kx, c):
            x, j = divmod(kx, 2)
            at = c * MODES + 8 * j
            return jnp.concatenate([parts[4 * x + y][at : at + 8] for y in range(4)], axis=0)

        for c in range(2):
            plus[0, c] = field(0, c)
            plus[4, c] = field(4, c)
            for f in range(1, 4):
                up, down = field(f, c), field(MX - f, c)
                plus[f, c] = up + down
                less[f, c] = up - down

    base = (place[0] * LX + step * X_STEP) * 8
    tab = table[0]
    for j in range(0, X_STEP, 2):
        pair = []
        for k in (j, j + 1):
            real, imag = plus[0, 0], plus[0, 1]
            for f in range(1, 5):
                cos = phase[base + 8 * k + 2 * f - 2]
                sin = phase[base + 8 * k + 2 * f - 1]
                if f < 4:
                    real += plus[f, 0] * cos - less[f, 1] * sin
                    imag += plus[f, 1] * cos + less[f, 0] * sin
                else:
                    real += plus[4, 0] * cos + plus[4, 1] * sin
                    imag += plus[4, 1] * cos - plus[4, 0] * sin
            field_ = jnp.concatenate([real, imag], axis=0)
            high = field_.astype(bf16)
            low = (field_ - high.astype(f32)).astype(bf16)
            pair.append(jnp.concatenate([high, high, low], axis=0))
        both = jnp.dot(tab, jnp.concatenate(pair, axis=1), preferred_element_type=f32)
        both = both.astype(bf16)
        out[j] = both[:, :CI]
        out[j + 1] = both[:, CI:]


def synthesise(place, modes):
    return pl.pallas_call(
        synthesise_kernel,
        out_shape=jax.ShapeDtypeStruct((LX, CELLS, CI), bf16),
        grid_spec=pltpu.PrefetchScalarGridSpec(
            num_scalar_prefetch=1,
            grid=(LX // X_STEP,),
            in_specs=[
                pl.BlockSpec((GROUP, 2 * MODES, CI), lambda i, p: (0, 0, 0)),
                pl.BlockSpec((1, CELLS, 6 * ROWS), lambda i, p: (p[1], 0, 0)),
                pl.BlockSpec(memory_space=pltpu.SMEM),
            ],
            out_specs=pl.BlockSpec((X_STEP, CELLS, CI), lambda i, p: (i, 0, 0)),
            scratch_shapes=[
                pltpu.VMEM((5, 2, ROWS, CI), f32),
                pltpu.VMEM((4, 2, ROWS, CI), f32),
            ],
        ),
        compiler_params=pltpu.CompilerParams(vmem_limit_bytes=24 * 2**20),
        name="synthesise",
    )(place, modes, jnp.asarray(synthesise_tables()), jnp.asarray(x_phases()))


def adam_kernel(cot, got, master, moment1, moment2, new_master, new_moment1, new_moment2):
    rows, cols = SNAPS * MODES, 2 * OWN * MODES
    spec = got[...][:, cols:].astype(f32)
    spread = jnp.broadcast_to(spec[:, None, :], (SNAPS, MODES, cols)).reshape(rows, cols)
    spread = jnp.where(own_mode(rows, cols), spread, 0.0).astype(bf16)
    products = lax.dot_general(
        spread, cot[...].reshape(rows, 2 * CO), (((0,), (0,)), ((), ())), preferred_element_type=f32
    ).reshape(OWN, 2, MODES, 2 * CO)
    real = products[:, 0, :, :CO] + products[:, 1, :, CO:]
    imag = products[:, 0, :, CO:] - products[:, 1, :, :CO]
    grad = jnp.stack([real, imag], axis=1).reshape(cols, CO)
    first = beta_one * moment1[...] + (1.0 - beta_one) * grad
    second = beta_two * moment2[...] + (1.0 - beta_two) * grad * grad
    first_fix = 1.0 - beta_one**STEP
    second_fix = 1.0 - beta_two**STEP
    new_moment1[...] = first
    new_moment2[...] = second
    new_master[...] = master[...] - learn_rate * (first / first_fix) / (
        jnp.sqrt(second / second_fix) + epsilon
    )


def adam(cot, got, master, moment1, moment2):
    whole = pl.BlockSpec(memory_space=pltpu.VMEM)
    return pl.pallas_call(
        adam_kernel,
        out_shape=[jax.ShapeDtypeStruct(master.shape, f32)] * 3,
        in_specs=[whole] * 5,
        out_specs=[whole] * 3,
        compiler_params=pltpu.CompilerParams(vmem_limit_bytes=24 * 2**20),
        name="adam",
    )(cot, got, master, moment1, moment2)


def shards(cotangent, spectrum, master, moment1, moment2):
    place = jnp.stack([lax.axis_index("sx"), lax.axis_index("sy")]).astype(jnp.int32)
    partial = analyse(place, cotangent.reshape(LX, CELLS, CO))
    partial = lax.all_to_all(partial, ("sx", "sy"), 0, 0, tiled=True)
    scale = norm * np.tile(np.array([1.0, 2.0, 2.0, 2.0], np.float32), MODES // MZ)
    spectral_cot = (partial.astype(f32).sum(axis=0) * scale[:, None]).astype(bf16)
    every_cot = jnp.broadcast_to(spectral_cot[None], (SNAPS, MODES, 2 * CO))
    every_cot = lax.all_to_all(every_cot, "dp", 0, 0, tiled=True)
    state = (2 * OWN * MODES, CO)
    weight = master.reshape(state)
    got = mix(every_cot, weight, spectrum.reshape(2 * MODES, CI))
    got = lax.all_to_all(got, "dp", 0, 0, tiled=True)
    modes = lax.all_to_all(turn(got), ("sx", "sy"), 0, 0, tiled=True)
    input_grad = synthesise(place, modes).reshape(cotangent.shape)
    states = adam(every_cot, got, weight, moment1.reshape(state), moment2.reshape(state))
    return (input_grad, *(s.reshape(master.shape) for s in states))


def solution(mesh):
    grid = P("dp", "sx", "sy", None, None)
    state = P("dp", None, "sx", "sy", None, None)
    in_specs = (grid, P(None, "dp", "sx", "sy", None, None), state, state, state)
    out_specs = (grid, state, state, state)
    return jax.shard_map(shards, mesh=mesh, in_specs=in_specs, out_specs=out_specs, check_vma=False)
```

```python
import math

import jax
import jax.numpy as jnp
import ml_dtypes
import numpy as np
from jax import lax
from jax.experimental import pallas as pl
from jax.experimental.pallas import tpu as pltpu
from jax.sharding import PartitionSpec as P

NX = 48
NY = 48
NZ = 48
MX = 8
MY = 8
MZ = 4
CI = 128
CO = 128
STEP = 100

beta_one = 0.9
beta_two = 0.95
learn_rate = 0.001
epsilon = 1e-08
norm = 1.0 / math.sqrt(NX * NY * NZ)

LX = 12
LY = 12
CELLS = LY * NZ
ROWS = MY * MZ
MODES = 16
GROUP = 16
SNAPS = 32
OWN = 4
CHUNK = 4

bf16 = jnp.bfloat16
f32 = jnp.float32


def freqs(count):
    index = np.arange(count)
    return np.where(index < count // 2, index, index - count)


def angles(places, numbers, length):
    return 2.0 * np.pi * ((places[:, None] * numbers[None, :]) % length) / length


def narrow(table):
    return table.astype(np.float32).astype(ml_dtypes.bfloat16)


def high_low(table):
    high = narrow(table)
    return high, narrow(table - high.astype(np.float64))


def x_phase(f, x):
    theta = 2.0 * math.pi * (f * x % NX) / NX
    return math.cos(theta), math.sin(theta)


def analyse_table():
    z_angle = angles(np.arange(NZ), np.arange(MZ), NZ)
    z_cos = narrow(np.cos(z_angle)).astype(np.float64)
    z_sin = narrow(-np.sin(z_angle)).astype(np.float64)
    y_angle = angles(np.arange(LY), freqs(MY), NY)
    y_cos, y_sin = np.cos(y_angle), np.sin(y_angle)
    real = np.einsum("ym,zl->mlyz", y_cos, z_cos) + np.einsum("ym,zl->mlyz", y_sin, z_sin)
    imag = np.einsum("ym,zl->mlyz", y_cos, z_sin) - np.einsum("ym,zl->mlyz", y_sin, z_cos)
    return np.concatenate(high_low(np.stack([real, imag]).reshape(2 * ROWS, CELLS)), axis=0)


def synthesise_table():
    z_angle = angles(np.arange(NZ), np.arange(MZ), NZ)
    y_angle = angles(np.arange(LY), freqs(MY), NY)
    theta = y_angle[:, None, :, None] + z_angle[None, :, None, :]
    table = norm * np.stack([np.cos(theta), -np.sin(theta)], axis=2)
    high, low = high_low(table.reshape(CELLS, 2 * ROWS))
    return np.concatenate([high, low, high], axis=1)


def quarter_turns(place, kx):
    row = lax.broadcasted_iota(jnp.int32, (ROWS, CO), 0) // MZ
    ky = jnp.where(row < MY // 2, row, row - MY)
    turns = (ky * place[1] + int(freqs(MX)[kx]) * place[0]) & 3
    cos = jnp.where(turns == 0, 1.0, jnp.where(turns == 2, -1.0, 0.0))
    sin = jnp.where(turns == 1, 1.0, jnp.where(turns == 3, -1.0, 0.0))
    return cos, sin


def analyse_kernel(place, cot_hbm, table_hbm, out, cot, table, total, sems):
    chunks = LX // CHUNK
    copies = [pltpu.make_async_copy(table_hbm, table, sems.at[chunks])]
    for n in range(chunks):
        part = pl.ds(n * CHUNK, CHUNK)
        copies.append(pltpu.make_async_copy(cot_hbm.at[part], cot.at[part], sems.at[n]))
    for copy in copies:
        copy.start()
    copies[0].wait()
    for n in range(chunks):
        copies[1 + n].wait()
        real, imag = [], []
        for x in range(n * CHUNK, (n + 1) * CHUNK, 2):
            pair = jnp.concatenate([cot[x], cot[x + 1]], axis=1)
            both = jnp.dot(table[...], pair, preferred_element_type=f32)
            part = both[: 2 * ROWS] + both[2 * ROWS :]
            for lanes in (slice(0, CO), slice(CO, 2 * CO)):
                real.append(part[:ROWS, lanes])
                imag.append(part[ROWS:, lanes])

        def add(kx, c, value, n=n):
            total[kx, c] = value if n == 0 else total[kx, c] + value

        add(0, 0, sum(real))
        add(0, 1, sum(imag))
        for f in range(1, 5):
            rc = rs = ic = is_ = 0.0
            for j in range(CHUNK):
                cos, sin = x_phase(f, n * CHUNK + j)
                rc += real[j] * cos
                rs += real[j] * sin
                ic += imag[j] * cos
                is_ += imag[j] * sin
            if f < 4:
                add(f, 0, rc + is_)
                add(f, 1, ic - rs)
            add(MX - f, 0, rc - is_)
            add(MX - f, 1, ic + rs)
    for x in range(4):
        halves = []
        for j in range(2):
            cos, sin = quarter_turns(place, 2 * x + j)
            real, imag = total[2 * x + j, 0], total[2 * x + j, 1]
            halves.append((real * cos + imag * sin, imag * cos - real * sin))
        for y in range(4):
            for c in range(2):
                block = [half[c][8 * y : 8 * y + 8] for half in halves]
                out[4 * x + y, :, c * CO : (c + 1) * CO] = jnp.concatenate(block, axis=0).astype(bf16)


def in_hbm(array):
    return pltpu.with_memory_space_constraint(array, pltpu.HBM)


def analyse(place, cotangent):
    return pl.pallas_call(
        analyse_kernel,
        out_shape=jax.ShapeDtypeStruct((GROUP, MODES, 2 * CO), bf16),
        in_specs=[
            pl.BlockSpec(memory_space=pltpu.SMEM),
            pl.BlockSpec(memory_space=pltpu.HBM),
            pl.BlockSpec(memory_space=pltpu.HBM),
        ],
        out_specs=pl.BlockSpec(memory_space=pltpu.VMEM),
        scratch_shapes=[
            pltpu.VMEM((LX, CELLS, CO), bf16),
            pltpu.VMEM((4 * ROWS, CELLS), bf16),
            pltpu.VMEM((MX, 2, ROWS, CO), f32),
            pltpu.SemaphoreType.DMA((LX // CHUNK + 1,)),
        ],
        compiler_params=pltpu.CompilerParams(vmem_limit_bytes=24 * 2**20),
        name="analyse",
    )(place, in_hbm(cotangent), in_hbm(jnp.asarray(analyse_table())))


def own_mode(rows, cols):
    row = lax.broadcasted_iota(jnp.int32, (rows, cols), 0) % MODES
    return row == lax.broadcasted_iota(jnp.int32, (rows, cols), 1) % MODES


def channel_of(rows):
    row = lax.broadcasted_iota(jnp.int32, (rows, CI), 0)
    chan = lax.broadcasted_iota(jnp.int32, (rows, CI), 1)
    return jnp.where(chan == (row % SNAPS) * OWN + row // SNAPS, 1.0, 0.0).astype(bf16)


def mix_kernel(cot, master, spec, out):
    rows, cols = SNAPS * MODES, 2 * OWN * MODES
    weight = master[...].reshape(OWN, 2, MODES, CO)
    real, imag = weight[:, 0], weight[:, 1]
    table = jnp.concatenate(
        [
            jnp.stack([real, -imag], axis=1).reshape(cols, CO),
            jnp.stack([imag, real], axis=1).reshape(cols, CO),
        ],
        axis=1,
    ).astype(bf16)
    every = lax.dot_general(
        cot[...].reshape(rows, 2 * CO), table, (((1,), (1,)), ((), ())), preferred_element_type=f32
    )
    grad = jnp.where(own_mode(rows, cols), every, 0.0).reshape(SNAPS, MODES, cols).sum(axis=1)
    turned = lax.dot_general(
        channel_of(OWN * SNAPS), spec[...], (((1,), (1,)), ((), ())), preferred_element_type=f32
    )
    pieces = [turned[i * SNAPS : (i + 1) * SNAPS] for i in range(OWN)]
    out[:, 0, :] = grad.astype(bf16)
    out[:, 1, :] = jnp.concatenate(pieces, axis=1).astype(bf16)


def mix(cot, master, spec):
    return pl.pallas_call(
        mix_kernel,
        out_shape=jax.ShapeDtypeStruct((SNAPS, 2, 2 * OWN * MODES), bf16),
        in_specs=[pl.BlockSpec(memory_space=pltpu.VMEM)] * 3,
        out_specs=pl.BlockSpec(memory_space=pltpu.VMEM),
        compiler_params=pltpu.CompilerParams(vmem_limit_bytes=24 * 2**20),
        name="mix",
    )(cot, master, spec)


def turn_kernel(got, out):
    width = 2 * MODES
    grad = got[:, 0, :]
    stacked = jnp.concatenate([grad[:, i * width : (i + 1) * width] for i in range(OWN)], axis=0)
    turned = lax.dot_general(
        stacked, channel_of(OWN * SNAPS), (((0,), (0,)), ((), ())), preferred_element_type=f32
    )
    out[...] = jnp.broadcast_to(turned.astype(bf16)[None], out.shape)


def turn(got):
    return pl.pallas_call(
        turn_kernel,
        out_shape=jax.ShapeDtypeStruct((GROUP, 2 * MODES, CI), bf16),
        in_specs=[pl.BlockSpec(memory_space=pltpu.VMEM)],
        out_specs=pl.BlockSpec(memory_space=pltpu.VMEM),
        compiler_params=pltpu.CompilerParams(vmem_limit_bytes=24 * 2**20),
        name="turn",
    )(got)


def adam_step(cot, got, master, moment1, moment2):
    rows, cols = SNAPS * MODES, 2 * OWN * MODES
    spec = got[:, 1, :].astype(f32)
    spread = jnp.broadcast_to(spec[:, None, :], (SNAPS, MODES, cols)).reshape(rows, cols)
    spread = jnp.where(own_mode(rows, cols), spread, 0.0).astype(bf16)
    products = lax.dot_general(
        spread, cot[...].reshape(rows, 2 * CO), (((0,), (0,)), ((), ())), preferred_element_type=f32
    ).reshape(OWN, 2, MODES, 2 * CO)
    real = products[:, 0, :, :CO] + products[:, 1, :, CO:]
    imag = products[:, 0, :, CO:] - products[:, 1, :, :CO]
    grad = jnp.stack([real, imag], axis=1).reshape(cols, CO)
    first = beta_one * moment1[...] + (1.0 - beta_one) * grad
    second = beta_two * moment2[...] + (1.0 - beta_two) * grad * grad
    first_fix = 1.0 - beta_one**STEP
    second_fix = 1.0 - beta_two**STEP
    stepped = master[...] - learn_rate * (first / first_fix) / (
        jnp.sqrt(second / second_fix) + epsilon
    )
    return stepped, first, second


def finish_kernel(place, modes, table, cot, got, master, moment1, moment2, *refs):
    out_hbm, *states_hbm = refs[:4]
    out, states, plus, less, sems = refs[4:]
    parts = [modes[s].astype(f32) for s in range(GROUP)]

    def field(kx):
        x, j = divmod(kx, 2)
        real, imag = (
            jnp.concatenate(
                [parts[4 * x + y][c * MODES + 8 * j : c * MODES + 8 * j + 8] for y in range(4)], axis=0
            )
            for c in range(2)
        )
        cos, sin = quarter_turns(place, kx)
        return real * cos - imag * sin, imag * cos + real * sin

    for f in range(5):
        up = field(f)
        for c in range(2):
            plus[f, c] = up[c]
        if 0 < f < 4:
            down = field(MX - f)
            for c in range(2):
                plus[f, c] = up[c] + down[c]
                less[f, c] = up[c] - down[c]
    copies = []
    for x in range(0, LX, 2):
        pair = []
        for k in (x, x + 1):
            real, imag = plus[0, 0], plus[0, 1]
            for f in range(1, 5):
                cos, sin = x_phase(f, k)
                if f < 4:
                    real += plus[f, 0] * cos - less[f, 1] * sin
                    imag += plus[f, 1] * cos + less[f, 0] * sin
                else:
                    real += plus[4, 0] * cos + plus[4, 1] * sin
                    imag += plus[4, 1] * cos - plus[4, 0] * sin
            both = jnp.concatenate([real, imag], axis=0)
            high = both.astype(bf16)
            low = (both - high.astype(f32)).astype(bf16)
            pair.append(jnp.concatenate([high, high, low], axis=0))
        cells = jnp.dot(table[...], jnp.concatenate(pair, axis=1), preferred_element_type=f32)
        cells = cells.astype(bf16)
        out[x] = cells[:, :CI]
        out[x + 1] = cells[:, CI:]
        part = pl.ds(x, 2)
        copies.append(pltpu.make_async_copy(out.at[part], out_hbm.at[part], sems.at[x // 2]))
        copies[-1].start()
    for n, state in enumerate(adam_step(cot, got, master, moment1, moment2)):
        states[n] = state
        copies.append(pltpu.make_async_copy(states.at[n], states_hbm[n], sems.at[LX // 2 + n]))
        copies[-1].start()
    for copy in copies:
        copy.wait()


def finish(place, modes, cot, got, master, moment1, moment2):
    state = jax.ShapeDtypeStruct(master.shape, f32)
    return pl.pallas_call(
        finish_kernel,
        out_shape=[jax.ShapeDtypeStruct((LX, CELLS, CI), bf16), state, state, state],
        in_specs=[pl.BlockSpec(memory_space=pltpu.SMEM)]
        + [pl.BlockSpec(memory_space=pltpu.VMEM)] * 7,
        out_specs=[pl.BlockSpec(memory_space=pltpu.HBM)] * 4,
        scratch_shapes=[
            pltpu.VMEM((LX, CELLS, CI), bf16),
            pltpu.VMEM((3,) + master.shape, f32),
            pltpu.VMEM((5, 2, ROWS, CI), f32),
            pltpu.VMEM((4, 2, ROWS, CI), f32),
            pltpu.SemaphoreType.DMA((LX // 2 + 3,)),
        ],
        compiler_params=pltpu.CompilerParams(vmem_limit_bytes=24 * 2**20),
        name="finish",
    )(place, modes, jnp.asarray(synthesise_table()), cot, got, master, moment1, moment2)


def shards(cotangent, spectrum, master, moment1, moment2):
    place = jnp.stack([lax.axis_index("sx"), lax.axis_index("sy")]).astype(jnp.int32)
    partial = analyse(place, cotangent.reshape(LX, CELLS, CO))
    partial = lax.all_to_all(partial, ("sx", "sy"), 0, 0, tiled=True)
    scale = norm * np.tile(np.array([1.0, 2.0, 2.0, 2.0], np.float32), MODES // MZ)
    spectral_cot = (partial.astype(f32).sum(axis=0) * scale[:, None]).astype(bf16)
    every_cot = jnp.broadcast_to(spectral_cot[None], (SNAPS, MODES, 2 * CO))
    every_cot = lax.all_to_all(every_cot, "dp", 0, 0, tiled=True)
    state = (2 * OWN * MODES, CO)
    weight = master.reshape(state)
    got = mix(every_cot, weight, spectrum.reshape(2 * MODES, CI))
    got = lax.all_to_all(got, "dp", 0, 0, tiled=True)
    modes = lax.all_to_all(turn(got), ("sx", "sy"), 0, 0, tiled=True)
    input_grad, *states = finish(
        place, modes, every_cot, got, weight, moment1.reshape(state), moment2.reshape(state)
    )
    return (input_grad.reshape(cotangent.shape), *(s.reshape(master.shape) for s in states))


def solution(mesh):
    grid = P("dp", "sx", "sy", None, None)
    state = P("dp", None, "sx", "sy", None, None)
    in_specs = (grid, P(None, "dp", "sx", "sy", None, None), state, state, state)
    out_specs = (grid, state, state, state)
    return jax.shard_map(shards, mesh=mesh, in_specs=in_specs, out_specs=out_specs, check_vma=False)
```

```python
import math

import jax
import jax.numpy as jnp
import ml_dtypes
import numpy as np
from jax import lax
from jax.experimental import pallas as pl
from jax.experimental.pallas import tpu as pltpu
from jax.sharding import PartitionSpec as P

NX = 48
NY = 48
NZ = 48
MX = 8
MY = 8
MZ = 4
CI = 128
CO = 128
STEP = 100

beta_one = 0.9
beta_two = 0.95
learn_rate = 0.001
epsilon = 1e-08
norm = 1.0 / math.sqrt(NX * NY * NZ)

LX = 12
LY = 12
CELLS = LY * NZ
ROWS = MY * MZ
MODES = 16
GROUP = 16
SNAPS = 32
OWN = 4
CHUNK = 4

bf16 = jnp.bfloat16
f32 = jnp.float32


def freqs(count):
    index = np.arange(count)
    return np.where(index < count // 2, index, index - count)


def angles(places, numbers, length):
    return 2.0 * np.pi * ((places[:, None] * numbers[None, :]) % length) / length


def narrow(table):
    return table.astype(np.float32).astype(ml_dtypes.bfloat16)


def high_low(table):
    high = narrow(table)
    return high, narrow(table - high.astype(np.float64))


def x_phase(f, x):
    theta = 2.0 * math.pi * (f * x % NX) / NX
    return math.cos(theta), math.sin(theta)


def analyse_table():
    z_angle = angles(np.arange(NZ), np.arange(MZ), NZ)
    z_cos = narrow(np.cos(z_angle)).astype(np.float64)
    z_sin = narrow(-np.sin(z_angle)).astype(np.float64)
    y_angle = angles(np.arange(LY), freqs(MY), NY)
    y_cos, y_sin = np.cos(y_angle), np.sin(y_angle)
    real = np.einsum("ym,zl->mlyz", y_cos, z_cos) + np.einsum("ym,zl->mlyz", y_sin, z_sin)
    imag = np.einsum("ym,zl->mlyz", y_cos, z_sin) - np.einsum("ym,zl->mlyz", y_sin, z_cos)
    scale = norm * np.where(np.arange(MZ) > 0, 2.0, 1.0)[:, None, None]
    table = (np.stack([real, imag]) * scale).reshape(2 * ROWS, CELLS)
    return np.concatenate(high_low(table), axis=0)


def synthesise_table():
    z_angle = angles(np.arange(NZ), np.arange(MZ), NZ)
    y_angle = angles(np.arange(LY), freqs(MY), NY)
    theta = y_angle[:, None, :, None] + z_angle[None, :, None, :]
    table = norm * np.stack([np.cos(theta), -np.sin(theta)], axis=2)
    high, low = high_low(table.reshape(CELLS, 2 * ROWS))
    return np.concatenate([high, low, high], axis=1)


def quarter_turns(place, kx):
    row = lax.broadcasted_iota(jnp.int32, (ROWS, CO), 0) // MZ
    ky = jnp.where(row < MY // 2, row, row - MY)
    turns = (ky * place[1] + int(freqs(MX)[kx]) * place[0]) & 3
    cos = jnp.where(turns == 0, 1.0, jnp.where(turns == 2, -1.0, 0.0))
    sin = jnp.where(turns == 1, 1.0, jnp.where(turns == 3, -1.0, 0.0))
    return cos, sin


def analyse_kernel(place, cot_hbm, table_hbm, out, cot, table, total, sems):
    copies = [pltpu.make_async_copy(table_hbm, table, sems.at[0])]
    for n, part in enumerate((pl.ds(0, CHUNK), pl.ds(CHUNK, LX - CHUNK))):
        copies.append(pltpu.make_async_copy(cot_hbm.at[part], cot.at[part], sems.at[1 + n]))
    for copy in copies:
        copy.start()
    copies[0].wait()
    for n in range(LX // CHUNK):
        if n < 2:
            copies[1 + n].wait()
        real, imag = [], []
        for x in range(n * CHUNK, (n + 1) * CHUNK, 2):
            pair = jnp.concatenate([cot[x], cot[x + 1]], axis=1)
            both = jnp.dot(table[...], pair, preferred_element_type=f32)
            part = both[: 2 * ROWS] + both[2 * ROWS :]
            for lanes in (slice(0, CO), slice(CO, 2 * CO)):
                real.append(part[:ROWS, lanes])
                imag.append(part[ROWS:, lanes])

        def add(kx, c, value, n=n):
            total[kx, c] = value if n == 0 else total[kx, c] + value

        add(0, 0, sum(real))
        add(0, 1, sum(imag))
        for f in range(1, 5):
            rc = rs = ic = is_ = 0.0
            for j in range(CHUNK):
                cos, sin = x_phase(f, n * CHUNK + j)
                rc += real[j] * cos
                rs += real[j] * sin
                ic += imag[j] * cos
                is_ += imag[j] * sin
            if f < 4:
                add(f, 0, rc + is_)
                add(f, 1, ic - rs)
            add(MX - f, 0, rc - is_)
            add(MX - f, 1, ic + rs)
    for x in range(4):
        halves = []
        for j in range(2):
            cos, sin = quarter_turns(place, 2 * x + j)
            real, imag = total[2 * x + j, 0], total[2 * x + j, 1]
            halves.append((real * cos + imag * sin, imag * cos - real * sin))
        for y in range(4):
            for c in range(2):
                block = [half[c][8 * y : 8 * y + 8] for half in halves]
                out[4 * x + y, :, c * CO : (c + 1) * CO] = jnp.concatenate(block, axis=0).astype(bf16)


def in_hbm(array):
    return pltpu.with_memory_space_constraint(array, pltpu.HBM)


def analyse(place, cotangent):
    return pl.pallas_call(
        analyse_kernel,
        out_shape=jax.ShapeDtypeStruct((GROUP, MODES, 2 * CO), bf16),
        in_specs=[
            pl.BlockSpec(memory_space=pltpu.SMEM),
            pl.BlockSpec(memory_space=pltpu.HBM),
            pl.BlockSpec(memory_space=pltpu.HBM),
        ],
        out_specs=pl.BlockSpec(memory_space=pltpu.VMEM),
        scratch_shapes=[
            pltpu.VMEM((LX, CELLS, CO), bf16),
            pltpu.VMEM((4 * ROWS, CELLS), bf16),
            pltpu.VMEM((MX, 2, ROWS, CO), f32),
            pltpu.SemaphoreType.DMA((3,)),
        ],
        compiler_params=pltpu.CompilerParams(vmem_limit_bytes=24 * 2**20),
        name="analyse",
    )(place, in_hbm(cotangent), in_hbm(jnp.asarray(analyse_table())))


def own_mode(rows, cols):
    row = lax.broadcasted_iota(jnp.int32, (rows, cols), 0) % MODES
    return row == lax.broadcasted_iota(jnp.int32, (rows, cols), 1) % MODES


def channel_of(rows):
    row = lax.broadcasted_iota(jnp.int32, (rows, CI), 0)
    chan = lax.broadcasted_iota(jnp.int32, (rows, CI), 1)
    return jnp.where(chan == (row % SNAPS) * OWN + row // SNAPS, 1.0, 0.0).astype(bf16)


def mix_kernel(cot, master, spec, out):
    rows, cols = SNAPS * MODES, 2 * OWN * MODES
    weight = master[...].reshape(OWN, 2, MODES, CO)
    real, imag = weight[:, 0], weight[:, 1]
    table = jnp.concatenate(
        [
            jnp.stack([real, -imag], axis=1).reshape(cols, CO),
            jnp.stack([imag, real], axis=1).reshape(cols, CO),
        ],
        axis=1,
    ).astype(bf16)
    every = lax.dot_general(
        cot[...].reshape(rows, 2 * CO), table, (((1,), (1,)), ((), ())), preferred_element_type=f32
    )
    grad = jnp.where(own_mode(rows, cols), every, 0.0).reshape(SNAPS, MODES, cols).sum(axis=1)
    turned = lax.dot_general(
        channel_of(OWN * SNAPS), spec[...], (((1,), (1,)), ((), ())), preferred_element_type=f32
    )
    pieces = [turned[i * SNAPS : (i + 1) * SNAPS] for i in range(OWN)]
    out[:, 0, :] = grad.astype(bf16)
    out[:, 1, :] = jnp.concatenate(pieces, axis=1).astype(bf16)


def mix(cot, master, spec):
    return pl.pallas_call(
        mix_kernel,
        out_shape=jax.ShapeDtypeStruct((SNAPS, 2, 2 * OWN * MODES), bf16),
        in_specs=[pl.BlockSpec(memory_space=pltpu.VMEM)] * 3,
        out_specs=pl.BlockSpec(memory_space=pltpu.VMEM),
        compiler_params=pltpu.CompilerParams(vmem_limit_bytes=24 * 2**20),
        name="mix",
    )(cot, master, spec)


def turn_kernel(got, out):
    width = 2 * MODES
    grad = got[:, 0, :]
    stacked = jnp.concatenate([grad[:, i * width : (i + 1) * width] for i in range(OWN)], axis=0)
    turned = lax.dot_general(
        stacked, channel_of(OWN * SNAPS), (((0,), (0,)), ((), ())), preferred_element_type=f32
    )
    out[...] = jnp.broadcast_to(turned.astype(bf16)[None], out.shape)


def turn(got):
    return pl.pallas_call(
        turn_kernel,
        out_shape=jax.ShapeDtypeStruct((GROUP, 2 * MODES, CI), bf16),
        in_specs=[pl.BlockSpec(memory_space=pltpu.VMEM)],
        out_specs=pl.BlockSpec(memory_space=pltpu.VMEM),
        compiler_params=pltpu.CompilerParams(vmem_limit_bytes=24 * 2**20),
        name="turn",
    )(got)


def adam_step(cot, got, master, moment1, moment2):
    rows, cols = SNAPS * MODES, 2 * OWN * MODES
    spec = got[:, 1, :].astype(f32)
    spread = jnp.broadcast_to(spec[:, None, :], (SNAPS, MODES, cols)).reshape(rows, cols)
    spread = jnp.where(own_mode(rows, cols), spread, 0.0).astype(bf16)
    products = lax.dot_general(
        spread, cot[...].reshape(rows, 2 * CO), (((0,), (0,)), ((), ())), preferred_element_type=f32
    ).reshape(OWN, 2, MODES, 2 * CO)
    real = products[:, 0, :, :CO] + products[:, 1, :, CO:]
    imag = products[:, 0, :, CO:] - products[:, 1, :, :CO]
    grad = jnp.stack([real, imag], axis=1).reshape(cols, CO)
    first = beta_one * moment1[...] + (1.0 - beta_one) * grad
    second = beta_two * moment2[...] + (1.0 - beta_two) * grad * grad
    first_fix = 1.0 - beta_one**STEP
    second_fix = 1.0 - beta_two**STEP
    stepped = master[...] - learn_rate * (first / first_fix) / (
        jnp.sqrt(second / second_fix) + epsilon
    )
    return stepped, first, second


def finish_kernel(place, modes, table, cot, got, master, moment1, moment2, *refs):
    out_hbm, *states_hbm = refs[:4]
    out, states, plus, less, sems = refs[4:]
    parts = [modes[s].astype(f32) for s in range(GROUP)]

    def field(kx):
        x, j = divmod(kx, 2)
        real, imag = (
            jnp.concatenate(
                [parts[4 * x + y][c * MODES + 8 * j : c * MODES + 8 * j + 8] for y in range(4)], axis=0
            )
            for c in range(2)
        )
        cos, sin = quarter_turns(place, kx)
        return real * cos - imag * sin, imag * cos + real * sin

    for f in range(5):
        up = field(f)
        for c in range(2):
            plus[f, c] = up[c]
        if 0 < f < 4:
            down = field(MX - f)
            for c in range(2):
                plus[f, c] = up[c] + down[c]
                less[f, c] = up[c] - down[c]
    copies = []
    for x in range(0, LX, 2):
        pair = []
        for k in (x, x + 1):
            real, imag = plus[0, 0], plus[0, 1]
            for f in range(1, 5):
                cos, sin = x_phase(f, k)
                if f < 4:
                    real += plus[f, 0] * cos - less[f, 1] * sin
                    imag += plus[f, 1] * cos + less[f, 0] * sin
                else:
                    real += plus[4, 0] * cos + plus[4, 1] * sin
                    imag += plus[4, 1] * cos - plus[4, 0] * sin
            both = jnp.concatenate([real, imag], axis=0)
            high = both.astype(bf16)
            low = (both - high.astype(f32)).astype(bf16)
            pair.append(jnp.concatenate([high, high, low], axis=0))
        cells = jnp.dot(table[...], jnp.concatenate(pair, axis=1), preferred_element_type=f32)
        cells = cells.astype(bf16)
        out[x] = cells[:, :CI]
        out[x + 1] = cells[:, CI:]
        part = pl.ds(x, 2)
        copies.append(pltpu.make_async_copy(out.at[part], out_hbm.at[part], sems.at[x // 2]))
        copies[-1].start()
    for n, state in enumerate(adam_step(cot, got, master, moment1, moment2)):
        states[n] = state
        copies.append(pltpu.make_async_copy(states.at[n], states_hbm[n], sems.at[LX // 2 + n]))
        copies[-1].start()
    for copy in copies:
        copy.wait()


def finish(place, modes, cot, got, master, moment1, moment2):
    state = jax.ShapeDtypeStruct(master.shape, f32)
    return pl.pallas_call(
        finish_kernel,
        out_shape=[jax.ShapeDtypeStruct((LX, CELLS, CI), bf16), state, state, state],
        in_specs=[pl.BlockSpec(memory_space=pltpu.SMEM)]
        + [pl.BlockSpec(memory_space=pltpu.VMEM)] * 7,
        out_specs=[pl.BlockSpec(memory_space=pltpu.HBM)] * 4,
        scratch_shapes=[
            pltpu.VMEM((LX, CELLS, CI), bf16),
            pltpu.VMEM((3,) + master.shape, f32),
            pltpu.VMEM((5, 2, ROWS, CI), f32),
            pltpu.VMEM((4, 2, ROWS, CI), f32),
            pltpu.SemaphoreType.DMA((LX // 2 + 3,)),
        ],
        compiler_params=pltpu.CompilerParams(vmem_limit_bytes=24 * 2**20),
        name="finish",
    )(place, modes, jnp.asarray(synthesise_table()), cot, got, master, moment1, moment2)


def shards(cotangent, spectrum, master, moment1, moment2):
    place = jnp.stack([lax.axis_index("sx"), lax.axis_index("sy")]).astype(jnp.int32)
    partial = analyse(place, cotangent.reshape(LX, CELLS, CO))
    partial = lax.all_to_all(partial, ("sx", "sy"), 0, 0, tiled=True)
    spectral_cot = partial.astype(f32).sum(axis=0).astype(bf16)
    every_cot = jnp.broadcast_to(spectral_cot[None], (SNAPS, MODES, 2 * CO))
    every_cot = lax.all_to_all(every_cot, "dp", 0, 0, tiled=True)
    state = (2 * OWN * MODES, CO)
    weight = master.reshape(state)
    got = mix(every_cot, weight, spectrum.reshape(2 * MODES, CI))
    got = lax.all_to_all(got, "dp", 0, 0, tiled=True)
    modes = lax.all_to_all(turn(got), ("sx", "sy"), 0, 0, tiled=True)
    input_grad, *states = finish(
        place, modes, every_cot, got, weight, moment1.reshape(state), moment2.reshape(state)
    )
    return (input_grad.reshape(cotangent.shape), *(s.reshape(master.shape) for s in states))


def solution(mesh):
    grid = P("dp", "sx", "sy", None, None)
    state = P("dp", None, "sx", "sy", None, None)
    in_specs = (grid, P(None, "dp", "sx", "sy", None, None), state, state, state)
    out_specs = (grid, state, state, state)
    return jax.shard_map(shards, mesh=mesh, in_specs=in_specs, out_specs=out_specs, check_vma=False)
```

```python
import math

import jax
import jax.numpy as jnp
import ml_dtypes
import numpy as np
from jax import lax
from jax.experimental import pallas as pl
from jax.experimental.pallas import tpu as pltpu
from jax.sharding import PartitionSpec as P

NX = 48
NY = 48
NZ = 48
MX = 8
MY = 8
MZ = 4
CI = 128
CO = 128
STEP = 100

beta_one = 0.9
beta_two = 0.95
learn_rate = 0.001
epsilon = 1e-08
norm = 1.0 / math.sqrt(NX * NY * NZ)

LX = 12
LY = 12
CELLS = LY * NZ
ROWS = MY * MZ
MODES = 16
GROUP = 16
SNAPS = 32
OWN = 4
CORES = 2
CHUNK = 4

bf16 = jnp.bfloat16
f32 = jnp.float32


def freqs(count):
    index = np.arange(count)
    return np.where(index < count // 2, index, index - count)


def angles(places, numbers, length):
    return 2.0 * np.pi * ((places[:, None] * numbers[None, :]) % length) / length


def narrow(table):
    return table.astype(np.float32).astype(ml_dtypes.bfloat16)


def high_low(table):
    high = narrow(table)
    return high, narrow(table - high.astype(np.float64))


def x_phase(f, x):
    theta = 2.0 * math.pi * (f * x % NX) / NX
    return math.cos(theta), math.sin(theta)


def analyse_table():
    z_angle = angles(np.arange(NZ), np.arange(MZ), NZ)
    z_cos = narrow(np.cos(z_angle)).astype(np.float64)
    z_sin = narrow(-np.sin(z_angle)).astype(np.float64)
    y_angle = angles(np.arange(LY), freqs(MY), NY)
    y_cos, y_sin = np.cos(y_angle), np.sin(y_angle)
    real = np.einsum("ym,zl->mlyz", y_cos, z_cos) + np.einsum("ym,zl->mlyz", y_sin, z_sin)
    imag = np.einsum("ym,zl->mlyz", y_cos, z_sin) - np.einsum("ym,zl->mlyz", y_sin, z_cos)
    scale = norm * np.where(np.arange(MZ) > 0, 2.0, 1.0)[:, None, None]
    table = (np.stack([real, imag]) * scale).reshape(2 * ROWS, CELLS)
    return np.concatenate(high_low(table), axis=0)


def synthesise_table():
    z_angle = angles(np.arange(NZ), np.arange(MZ), NZ)
    y_angle = angles(np.arange(LY), freqs(MY), NY)
    theta = y_angle[:, None, :, None] + z_angle[None, :, None, :]
    table = norm * np.stack([np.cos(theta), -np.sin(theta)], axis=2)
    high, low = high_low(table.reshape(CELLS, 2 * ROWS))
    return np.concatenate([high, low, high], axis=1)


def quarter_turns(place, kx):
    row = lax.broadcasted_iota(jnp.int32, (ROWS, CO), 0) // MZ
    ky = jnp.where(row < MY // 2, row, row - MY)
    turns = (ky * place[1] + int(freqs(MX)[kx]) * place[0]) & 3
    cos = jnp.where(turns == 0, 1.0, jnp.where(turns == 2, -1.0, 0.0))
    sin = jnp.where(turns == 1, 1.0, jnp.where(turns == 3, -1.0, 0.0))
    return cos, sin


def analyse_kernel(place, cot_hbm, table_hbm, out, cot, table, total, sems):
    copies = [pltpu.make_async_copy(table_hbm, table, sems.at[0])]
    for n, part in enumerate((pl.ds(0, CHUNK), pl.ds(CHUNK, LX - CHUNK))):
        copies.append(pltpu.make_async_copy(cot_hbm.at[part], cot.at[part], sems.at[1 + n]))
    for copy in copies:
        copy.start()
    copies[0].wait()
    for n in range(LX // CHUNK):
        if n < 2:
            copies[1 + n].wait()
        real, imag = [], []
        for x in range(n * CHUNK, (n + 1) * CHUNK, 2):
            pair = jnp.concatenate([cot[x], cot[x + 1]], axis=1)
            both = jnp.dot(table[...], pair, preferred_element_type=f32)
            part = both[: 2 * ROWS] + both[2 * ROWS :]
            for lanes in (slice(0, CO), slice(CO, 2 * CO)):
                real.append(part[:ROWS, lanes])
                imag.append(part[ROWS:, lanes])

        def add(kx, c, value, n=n):
            total[kx, c] = value if n == 0 else total[kx, c] + value

        add(0, 0, sum(real))
        add(0, 1, sum(imag))
        for f in range(1, 5):
            rc = rs = ic = is_ = 0.0
            for j in range(CHUNK):
                cos, sin = x_phase(f, n * CHUNK + j)
                rc += real[j] * cos
                rs += real[j] * sin
                ic += imag[j] * cos
                is_ += imag[j] * sin
            if f < 4:
                add(f, 0, rc + is_)
                add(f, 1, ic - rs)
            add(MX - f, 0, rc - is_)
            add(MX - f, 1, ic + rs)
    for x in range(4):
        halves = []
        for j in range(2):
            cos, sin = quarter_turns(place, 2 * x + j)
            real, imag = total[2 * x + j, 0], total[2 * x + j, 1]
            halves.append((real * cos + imag * sin, imag * cos - real * sin))
        for y in range(4):
            for c in range(2):
                block = [half[c][8 * y : 8 * y + 8] for half in halves]
                out[4 * x + y, :, c * CO : (c + 1) * CO] = jnp.concatenate(block, axis=0).astype(bf16)


def in_hbm(array):
    return pltpu.with_memory_space_constraint(array, pltpu.HBM)


def analyse(place, cotangent):
    return pl.pallas_call(
        analyse_kernel,
        out_shape=jax.ShapeDtypeStruct((GROUP, MODES, 2 * CO), bf16),
        in_specs=[
            pl.BlockSpec(memory_space=pltpu.SMEM),
            pl.BlockSpec(memory_space=pltpu.HBM),
            pl.BlockSpec(memory_space=pltpu.HBM),
        ],
        out_specs=pl.BlockSpec(memory_space=pltpu.VMEM),
        scratch_shapes=[
            pltpu.VMEM((LX, CELLS, CO), bf16),
            pltpu.VMEM((4 * ROWS, CELLS), bf16),
            pltpu.VMEM((MX, 2, ROWS, CO), f32),
            pltpu.SemaphoreType.DMA((3,)),
        ],
        compiler_params=pltpu.CompilerParams(vmem_limit_bytes=24 * 2**20),
        name="analyse",
    )(place, in_hbm(cotangent), in_hbm(jnp.asarray(analyse_table())))


def own_mode(rows, cols):
    row = lax.broadcasted_iota(jnp.int32, (rows, cols), 0) % MODES
    return row == lax.broadcasted_iota(jnp.int32, (rows, cols), 1) % MODES


def channel_of(rows):
    row = lax.broadcasted_iota(jnp.int32, (rows, CI), 0)
    chan = lax.broadcasted_iota(jnp.int32, (rows, CI), 1)
    return jnp.where(chan == (row % SNAPS) * OWN + row // SNAPS, 1.0, 0.0).astype(bf16)


def mix_kernel(cot, master, spec, out):
    rows, cols = SNAPS * MODES, 2 * OWN * MODES
    weight = master[...].reshape(OWN, 2, MODES, CO)
    real, imag = weight[:, 0], weight[:, 1]
    table = jnp.concatenate(
        [
            jnp.stack([real, -imag], axis=1).reshape(cols, CO),
            jnp.stack([imag, real], axis=1).reshape(cols, CO),
        ],
        axis=1,
    ).astype(bf16)
    every = lax.dot_general(
        cot[...].reshape(rows, 2 * CO), table, (((1,), (1,)), ((), ())), preferred_element_type=f32
    )
    grad = jnp.where(own_mode(rows, cols), every, 0.0).reshape(SNAPS, MODES, cols).sum(axis=1)
    turned = lax.dot_general(
        channel_of(OWN * SNAPS), spec[...], (((1,), (1,)), ((), ())), preferred_element_type=f32
    )
    pieces = [turned[i * SNAPS : (i + 1) * SNAPS] for i in range(OWN)]
    grad, sent = grad.astype(bf16), jnp.concatenate(pieces, axis=1).astype(bf16)
    for core in range(CORES):
        out[:, core, 0, :] = grad
        out[:, core, 1, :] = sent


def mix(cot, master, spec):
    return pl.pallas_call(
        mix_kernel,
        out_shape=jax.ShapeDtypeStruct((SNAPS, CORES, 2, 2 * OWN * MODES), bf16),
        in_specs=[pl.BlockSpec(memory_space=pltpu.VMEM)] * 3,
        out_specs=pl.BlockSpec(memory_space=pltpu.VMEM),
        compiler_params=pltpu.CompilerParams(vmem_limit_bytes=24 * 2**20),
        name="mix",
    )(cot, master, spec)


def turn_kernel(got, out):
    width = 2 * MODES
    for core in range(CORES):
        grad = got[:, core, 0, :]
        stacked = jnp.concatenate([grad[:, i * width : (i + 1) * width] for i in range(OWN)], axis=0)
        turned = lax.dot_general(
            stacked, channel_of(OWN * SNAPS), (((0,), (0,)), ((), ())), preferred_element_type=f32
        )
        shape = (GROUP // CORES, width, CI)
        out[:, core * width : (core + 1) * width, :] = jnp.broadcast_to(turned.astype(bf16)[None], shape)


def turn(got):
    return pl.pallas_call(
        turn_kernel,
        out_shape=jax.ShapeDtypeStruct((GROUP // CORES, CORES * 2 * MODES, CI), bf16),
        in_specs=[pl.BlockSpec(memory_space=pltpu.VMEM)],
        out_specs=pl.BlockSpec(memory_space=pltpu.VMEM),
        compiler_params=pltpu.CompilerParams(vmem_limit_bytes=24 * 2**20),
        name="turn",
    )(got)


def adam_step(place, cot, got, master, moment1, moment2):
    rows, cols = SNAPS * MODES, 2 * OWN * MODES
    spec = jnp.where(place[1] % CORES == 0, got[:, 0, 1, :].astype(f32), got[:, 1, 1, :].astype(f32))
    spread = jnp.broadcast_to(spec[:, None, :], (SNAPS, MODES, cols)).reshape(rows, cols)
    spread = jnp.where(own_mode(rows, cols), spread, 0.0).astype(bf16)
    products = lax.dot_general(
        spread, cot[...].reshape(rows, 2 * CO), (((0,), (0,)), ((), ())), preferred_element_type=f32
    ).reshape(OWN, 2, MODES, 2 * CO)
    real = products[:, 0, :, :CO] + products[:, 1, :, CO:]
    imag = products[:, 0, :, CO:] - products[:, 1, :, :CO]
    grad = jnp.stack([real, imag], axis=1).reshape(cols, CO)
    first = beta_one * moment1[...] + (1.0 - beta_one) * grad
    second = beta_two * moment2[...] + (1.0 - beta_two) * grad * grad
    first_fix = 1.0 - beta_one**STEP
    second_fix = 1.0 - beta_two**STEP
    stepped = master[...] - learn_rate * (first / first_fix) / (
        jnp.sqrt(second / second_fix) + epsilon
    )
    return stepped, first, second


def finish_kernel(place, modes, table, cot, got, master, moment1, moment2, *refs):
    out_hbm, *states_hbm = refs[:4]
    out, states, plus, less, sems = refs[4:]
    width = 2 * MODES
    parts = [
        modes[s // CORES, s % CORES * width : (s % CORES + 1) * width].astype(f32) for s in range(GROUP)
    ]

    def field(kx):
        x, j = divmod(kx, 2)
        real, imag = (
            jnp.concatenate(
                [parts[4 * x + y][c * MODES + 8 * j : c * MODES + 8 * j + 8] for y in range(4)], axis=0
            )
            for c in range(2)
        )
        cos, sin = quarter_turns(place, kx)
        return real * cos - imag * sin, imag * cos + real * sin

    for f in range(5):
        up = field(f)
        for c in range(2):
            plus[f, c] = up[c]
        if 0 < f < 4:
            down = field(MX - f)
            for c in range(2):
                plus[f, c] = up[c] + down[c]
                less[f, c] = up[c] - down[c]
    copies = []
    for x in range(0, LX, 2):
        pair = []
        for k in (x, x + 1):
            real, imag = plus[0, 0], plus[0, 1]
            for f in range(1, 5):
                cos, sin = x_phase(f, k)
                if f < 4:
                    real += plus[f, 0] * cos - less[f, 1] * sin
                    imag += plus[f, 1] * cos + less[f, 0] * sin
                else:
                    real += plus[4, 0] * cos + plus[4, 1] * sin
                    imag += plus[4, 1] * cos - plus[4, 0] * sin
            both = jnp.concatenate([real, imag], axis=0)
            high = both.astype(bf16)
            low = (both - high.astype(f32)).astype(bf16)
            pair.append(jnp.concatenate([high, high, low], axis=0))
        cells = jnp.dot(table[...], jnp.concatenate(pair, axis=1), preferred_element_type=f32)
        cells = cells.astype(bf16)
        out[x] = cells[:, :CI]
        out[x + 1] = cells[:, CI:]
        part = pl.ds(x, 2)
        copies.append(pltpu.make_async_copy(out.at[part], out_hbm.at[part], sems.at[x // 2]))
        copies[-1].start()
    for n, state in enumerate(adam_step(place, cot, got, master, moment1, moment2)):
        states[n] = state
        copies.append(pltpu.make_async_copy(states.at[n], states_hbm[n], sems.at[LX // 2 + n]))
        copies[-1].start()
    for copy in copies:
        copy.wait()


def finish(place, modes, cot, got, master, moment1, moment2):
    state = jax.ShapeDtypeStruct(master.shape, f32)
    return pl.pallas_call(
        finish_kernel,
        out_shape=[jax.ShapeDtypeStruct((LX, CELLS, CI), bf16), state, state, state],
        in_specs=[pl.BlockSpec(memory_space=pltpu.SMEM)]
        + [pl.BlockSpec(memory_space=pltpu.VMEM)] * 7,
        out_specs=[pl.BlockSpec(memory_space=pltpu.HBM)] * 4,
        scratch_shapes=[
            pltpu.VMEM((LX, CELLS, CI), bf16),
            pltpu.VMEM((3,) + master.shape, f32),
            pltpu.VMEM((5, 2, ROWS, CI), f32),
            pltpu.VMEM((4, 2, ROWS, CI), f32),
            pltpu.SemaphoreType.DMA((LX // 2 + 3,)),
        ],
        compiler_params=pltpu.CompilerParams(vmem_limit_bytes=24 * 2**20),
        name="finish",
    )(place, modes, jnp.asarray(synthesise_table()), cot, got, master, moment1, moment2)


def planes():
    dp, core = np.arange(SNAPS)[:, None], np.arange(CORES)
    return [(4 * dp + CORES * half + core).reshape(-1).tolist() for half in range(2)]


def columns():
    return [list(range(core, GROUP, CORES)) for core in range(CORES)]


def shards(cotangent, spectrum, master, moment1, moment2):
    place = jnp.stack([lax.axis_index("sx"), lax.axis_index("sy")]).astype(jnp.int32)
    partial = analyse(place, cotangent.reshape(LX, CELLS, CO))
    partial = lax.all_to_all(partial, ("sx", "sy"), 0, 0, tiled=True)
    spectral_cot = partial.astype(f32).sum(axis=0).astype(bf16)
    every_cot = jnp.broadcast_to(spectral_cot[None], (SNAPS, MODES, 2 * CO))
    every_cot = lax.all_to_all(every_cot, "dp", 0, 0, tiled=True)
    state = (2 * OWN * MODES, CO)
    weight = master.reshape(state)
    got = mix(every_cot, weight, spectrum.reshape(2 * MODES, CI))
    got = got.reshape(SNAPS * CORES, 2, 2 * OWN * MODES)
    got = lax.all_to_all(got, ("dp", "sy"), 0, 0, tiled=True, axis_index_groups=planes())
    got = got.reshape(SNAPS, CORES, 2, 2 * OWN * MODES)
    modes = lax.all_to_all(turn(got), ("sx", "sy"), 0, 0, tiled=True, axis_index_groups=columns())
    input_grad, *states = finish(
        place, modes, every_cot, got, weight, moment1.reshape(state), moment2.reshape(state)
    )
    return (input_grad.reshape(cotangent.shape), *(s.reshape(master.shape) for s in states))


def solution(mesh):
    grid = P("dp", "sx", "sy", None, None)
    state = P("dp", None, "sx", "sy", None, None)
    in_specs = (grid, P(None, "dp", "sx", "sy", None, None), state, state, state)
    out_specs = (grid, state, state, state)
    return jax.shard_map(shards, mesh=mesh, in_specs=in_specs, out_specs=out_specs, check_vma=False)
```

```python
import math

import jax
import jax.numpy as jnp
import ml_dtypes
import numpy as np
from jax import lax
from jax.experimental import pallas as pl
from jax.experimental.pallas import tpu as pltpu
from jax.sharding import PartitionSpec as P

NX = 48
NY = 48
NZ = 48
MX = 8
MY = 8
MZ = 4
CI = 128
CO = 128
STEP = 100

beta_one = 0.9
beta_two = 0.95
learn_rate = 0.001
epsilon = 1e-08
norm = 1.0 / math.sqrt(NX * NY * NZ)

LX = 12
LY = 12
CELLS = LY * NZ
ROWS = MY * MZ
MODES = 16
GROUP = 16
SNAPS = 32
OWN = 4
CORES = 2
CHUNK = 4

bf16 = jnp.bfloat16
f32 = jnp.float32


def freqs(count):
    index = np.arange(count)
    return np.where(index < count // 2, index, index - count)


def angles(places, numbers, length):
    return 2.0 * np.pi * ((places[:, None] * numbers[None, :]) % length) / length


def narrow(table):
    return table.astype(np.float32).astype(ml_dtypes.bfloat16)


def high_low(table):
    high = narrow(table)
    return high, narrow(table - high.astype(np.float64))


def x_phase(f, x):
    theta = 2.0 * math.pi * (f * x % NX) / NX
    return math.cos(theta), math.sin(theta)


def analyse_table():
    z_angle = angles(np.arange(NZ), np.arange(MZ), NZ)
    z_cos = narrow(np.cos(z_angle)).astype(np.float64)
    z_sin = narrow(-np.sin(z_angle)).astype(np.float64)
    y_angle = angles(np.arange(LY), freqs(MY), NY)
    y_cos, y_sin = np.cos(y_angle), np.sin(y_angle)
    real = np.einsum("ym,zl->mlyz", y_cos, z_cos) + np.einsum("ym,zl->mlyz", y_sin, z_sin)
    imag = np.einsum("ym,zl->mlyz", y_cos, z_sin) - np.einsum("ym,zl->mlyz", y_sin, z_cos)
    scale = norm * np.where(np.arange(MZ) > 0, 2.0, 1.0)[:, None, None]
    table = (np.stack([real, imag]) * scale).reshape(2 * ROWS, CELLS)
    return np.concatenate(high_low(table), axis=0)


def synthesise_table():
    z_angle = angles(np.arange(NZ), np.arange(MZ), NZ)
    y_angle = angles(np.arange(LY), freqs(MY), NY)
    theta = y_angle[:, None, :, None] + z_angle[None, :, None, :]
    table = norm * np.stack([np.cos(theta), -np.sin(theta)], axis=2)
    high, low = high_low(table.reshape(CELLS, 2 * ROWS))
    return np.concatenate([high, low, high], axis=1)


def quarter_turns(place, kx):
    row = lax.broadcasted_iota(jnp.int32, (ROWS, CO), 0) // MZ
    ky = jnp.where(row < MY // 2, row, row - MY)
    turns = (ky * place[1] + int(freqs(MX)[kx]) * place[0]) & 3
    cos = jnp.where(turns == 0, 1.0, jnp.where(turns == 2, -1.0, 0.0))
    sin = jnp.where(turns == 1, 1.0, jnp.where(turns == 3, -1.0, 0.0))
    return cos, sin


def analyse_kernel(place, cot_hbm, table_hbm, out, cot, table, total, sems):
    copies = [pltpu.make_async_copy(table_hbm, table, sems.at[0])]
    for n, part in enumerate((pl.ds(0, CHUNK), pl.ds(CHUNK, LX - CHUNK))):
        copies.append(pltpu.make_async_copy(cot_hbm.at[part], cot.at[part], sems.at[1 + n]))
    for copy in copies:
        copy.start()
    copies[0].wait()
    for n in range(LX // CHUNK):
        if n < 2:
            copies[1 + n].wait()
        real, imag = [], []
        for x in range(n * CHUNK, (n + 1) * CHUNK, 2):
            pair = jnp.concatenate([cot[x], cot[x + 1]], axis=1)
            both = jnp.dot(table[...], pair, preferred_element_type=f32)
            part = both[: 2 * ROWS] + both[2 * ROWS :]
            for lanes in (slice(0, CO), slice(CO, 2 * CO)):
                real.append(part[:ROWS, lanes])
                imag.append(part[ROWS:, lanes])

        def add(kx, c, value, n=n):
            total[kx, c] = value if n == 0 else total[kx, c] + value

        add(0, 0, sum(real))
        add(0, 1, sum(imag))
        for f in range(1, 5):
            rc = rs = ic = is_ = 0.0
            for j in range(CHUNK):
                cos, sin = x_phase(f, n * CHUNK + j)
                rc += real[j] * cos
                rs += real[j] * sin
                ic += imag[j] * cos
                is_ += imag[j] * sin
            if f < 4:
                add(f, 0, rc + is_)
                add(f, 1, ic - rs)
            add(MX - f, 0, rc - is_)
            add(MX - f, 1, ic + rs)
    for x in range(4):
        halves = []
        for j in range(2):
            cos, sin = quarter_turns(place, 2 * x + j)
            real, imag = total[2 * x + j, 0], total[2 * x + j, 1]
            halves.append((real * cos + imag * sin, imag * cos - real * sin))
        for y in range(4):
            for c in range(2):
                block = [half[c][8 * y : 8 * y + 8] for half in halves]
                out[4 * x + y, :, c * CO : (c + 1) * CO] = jnp.concatenate(block, axis=0).astype(bf16)


def in_hbm(array):
    return pltpu.with_memory_space_constraint(array, pltpu.HBM)


def analyse(place, cotangent):
    return pl.pallas_call(
        analyse_kernel,
        out_shape=jax.ShapeDtypeStruct((GROUP, MODES, 2 * CO), bf16),
        in_specs=[
            pl.BlockSpec(memory_space=pltpu.SMEM),
            pl.BlockSpec(memory_space=pltpu.HBM),
            pl.BlockSpec(memory_space=pltpu.HBM),
        ],
        out_specs=pl.BlockSpec(memory_space=pltpu.VMEM),
        scratch_shapes=[
            pltpu.VMEM((LX, CELLS, CO), bf16),
            pltpu.VMEM((4 * ROWS, CELLS), bf16),
            pltpu.VMEM((MX, 2, ROWS, CO), f32),
            pltpu.SemaphoreType.DMA((3,)),
        ],
        compiler_params=pltpu.CompilerParams(vmem_limit_bytes=24 * 2**20),
        name="analyse",
    )(place, in_hbm(cotangent), in_hbm(jnp.asarray(analyse_table())))


def own_mode(rows, cols):
    row = lax.broadcasted_iota(jnp.int32, (rows, cols), 0) % MODES
    return row == lax.broadcasted_iota(jnp.int32, (rows, cols), 1) % MODES


def channel_of(rows):
    row = lax.broadcasted_iota(jnp.int32, (rows, CI), 0)
    chan = lax.broadcasted_iota(jnp.int32, (rows, CI), 1)
    return jnp.where(chan == (row % SNAPS) * OWN + row // SNAPS, 1.0, 0.0).astype(bf16)


def mix_kernel(cot, master, spec, out):
    rows, cols = SNAPS * MODES, 2 * OWN * MODES
    weight = master[...].reshape(OWN, 2, MODES, CO)
    real, imag = weight[:, 0], weight[:, 1]
    table = jnp.concatenate(
        [
            jnp.stack([real, -imag], axis=1).reshape(cols, CO),
            jnp.stack([imag, real], axis=1).reshape(cols, CO),
        ],
        axis=1,
    ).astype(bf16)
    every = lax.dot_general(
        cot[...].reshape(rows, 2 * CO), table, (((1,), (1,)), ((), ())), preferred_element_type=f32
    )
    grad = jnp.where(own_mode(rows, cols), every, 0.0).reshape(SNAPS, MODES, cols).sum(axis=1)
    turned = lax.dot_general(
        channel_of(OWN * SNAPS), spec[...], (((1,), (1,)), ((), ())), preferred_element_type=f32
    )
    pieces = [turned[i * SNAPS : (i + 1) * SNAPS] for i in range(OWN)]
    grad, sent = grad.astype(bf16), jnp.concatenate(pieces, axis=1).astype(bf16)
    for core in range(CORES):
        out[:, core, 0, :] = grad
        out[:, core, 1, :] = sent


def mix(cot, master, spec):
    return pl.pallas_call(
        mix_kernel,
        out_shape=jax.ShapeDtypeStruct((SNAPS, CORES, 2, 2 * OWN * MODES), bf16),
        in_specs=[pl.BlockSpec(memory_space=pltpu.VMEM)] * 3,
        out_specs=pl.BlockSpec(memory_space=pltpu.VMEM),
        compiler_params=pltpu.CompilerParams(vmem_limit_bytes=24 * 2**20),
        name="mix",
    )(cot, master, spec)


def turn_kernel(got, out):
    width = 2 * MODES
    for core in range(CORES):
        grad = got[:, core, 0, :]
        stacked = jnp.concatenate([grad[:, i * width : (i + 1) * width] for i in range(OWN)], axis=0)
        turned = lax.dot_general(
            stacked, channel_of(OWN * SNAPS), (((0,), (0,)), ((), ())), preferred_element_type=f32
        )
        shape = (GROUP // CORES, width, CI)
        out[:, core * width : (core + 1) * width, :] = jnp.broadcast_to(turned.astype(bf16)[None], shape)


def turn(got):
    return pl.pallas_call(
        turn_kernel,
        out_shape=jax.ShapeDtypeStruct((GROUP // CORES, CORES * 2 * MODES, CI), bf16),
        in_specs=[pl.BlockSpec(memory_space=pltpu.VMEM)],
        out_specs=pl.BlockSpec(memory_space=pltpu.VMEM),
        compiler_params=pltpu.CompilerParams(vmem_limit_bytes=24 * 2**20),
        name="turn",
    )(got)


def adam_step(place, cot, got, master, moment1, moment2):
    rows, cols = SNAPS * MODES, 2 * OWN * MODES
    spec = jnp.where(place[1] % CORES == 0, got[:, 0, 1, :].astype(f32), got[:, 1, 1, :].astype(f32))
    spread = jnp.broadcast_to(spec[:, None, :], (SNAPS, MODES, cols)).reshape(rows, cols)
    spread = jnp.where(own_mode(rows, cols), spread, 0.0).astype(bf16)
    products = lax.dot_general(
        spread, cot[...].reshape(rows, 2 * CO), (((0,), (0,)), ((), ())), preferred_element_type=f32
    ).reshape(OWN, 2, MODES, 2 * CO)
    real = products[:, 0, :, :CO] + products[:, 1, :, CO:]
    imag = products[:, 0, :, CO:] - products[:, 1, :, :CO]
    grad = jnp.stack([real, imag], axis=1).reshape(cols, CO)
    first = beta_one * moment1[...] + (1.0 - beta_one) * grad
    second = beta_two * moment2[...] + (1.0 - beta_two) * grad * grad
    first_fix = 1.0 - beta_one**STEP
    second_fix = 1.0 - beta_two**STEP
    stepped = master[...] - learn_rate * (first / first_fix) / (
        jnp.sqrt(second / second_fix) + epsilon
    )
    return stepped, first, second


def finish_kernel(place, modes, table, cot, got, master, moment1, moment2, *refs):
    out_hbm, *states_hbm = refs[:4]
    out, states, plus, less, sems = refs[4:]
    width = 2 * MODES
    parts = [
        modes[s % 4 // CORES * 4 + s // 4, s % CORES * width : (s % CORES + 1) * width].astype(f32)
        for s in range(GROUP)
    ]

    def field(kx):
        x, j = divmod(kx, 2)
        real, imag = (
            jnp.concatenate(
                [parts[4 * x + y][c * MODES + 8 * j : c * MODES + 8 * j + 8] for y in range(4)], axis=0
            )
            for c in range(2)
        )
        cos, sin = quarter_turns(place, kx)
        return real * cos - imag * sin, imag * cos + real * sin

    for f in range(5):
        up = field(f)
        for c in range(2):
            plus[f, c] = up[c]
        if 0 < f < 4:
            down = field(MX - f)
            for c in range(2):
                plus[f, c] = up[c] + down[c]
                less[f, c] = up[c] - down[c]
    copies = []
    for x in range(0, LX, 2):
        pair = []
        for k in (x, x + 1):
            real, imag = plus[0, 0], plus[0, 1]
            for f in range(1, 5):
                cos, sin = x_phase(f, k)
                if f < 4:
                    real += plus[f, 0] * cos - less[f, 1] * sin
                    imag += plus[f, 1] * cos + less[f, 0] * sin
                else:
                    real += plus[4, 0] * cos + plus[4, 1] * sin
                    imag += plus[4, 1] * cos - plus[4, 0] * sin
            both = jnp.concatenate([real, imag], axis=0)
            high = both.astype(bf16)
            low = (both - high.astype(f32)).astype(bf16)
            pair.append(jnp.concatenate([high, high, low], axis=0))
        cells = jnp.dot(table[...], jnp.concatenate(pair, axis=1), preferred_element_type=f32)
        cells = cells.astype(bf16)
        out[x] = cells[:, :CI]
        out[x + 1] = cells[:, CI:]
        part = pl.ds(x, 2)
        copies.append(pltpu.make_async_copy(out.at[part], out_hbm.at[part], sems.at[x // 2]))
        copies[-1].start()
    for n, state in enumerate(adam_step(place, cot, got, master, moment1, moment2)):
        states[n] = state
        copies.append(pltpu.make_async_copy(states.at[n], states_hbm[n], sems.at[LX // 2 + n]))
        copies[-1].start()
    for copy in copies:
        copy.wait()


def finish(place, modes, cot, got, master, moment1, moment2):
    state = jax.ShapeDtypeStruct(master.shape, f32)
    return pl.pallas_call(
        finish_kernel,
        out_shape=[jax.ShapeDtypeStruct((LX, CELLS, CI), bf16), state, state, state],
        in_specs=[pl.BlockSpec(memory_space=pltpu.SMEM)]
        + [pl.BlockSpec(memory_space=pltpu.VMEM)] * 7,
        out_specs=[pl.BlockSpec(memory_space=pltpu.HBM)] * 4,
        scratch_shapes=[
            pltpu.VMEM((LX, CELLS, CI), bf16),
            pltpu.VMEM((3,) + master.shape, f32),
            pltpu.VMEM((5, 2, ROWS, CI), f32),
            pltpu.VMEM((4, 2, ROWS, CI), f32),
            pltpu.SemaphoreType.DMA((LX // 2 + 3,)),
        ],
        compiler_params=pltpu.CompilerParams(vmem_limit_bytes=24 * 2**20),
        name="finish",
    )(place, modes, jnp.asarray(synthesise_table()), cot, got, master, moment1, moment2)


def planes():
    dp, core = np.arange(SNAPS)[:, None], np.arange(CORES)
    return [(4 * dp + CORES * half + core).reshape(-1).tolist() for half in range(2)]


def columns():
    half, run = np.arange(2)[:, None], np.arange(4)
    return [(4 * run + CORES * half + core).reshape(-1).tolist() for core in range(CORES)]


def shards(cotangent, spectrum, master, moment1, moment2):
    place = jnp.stack([lax.axis_index("sx"), lax.axis_index("sy")]).astype(jnp.int32)
    partial = analyse(place, cotangent.reshape(LX, CELLS, CO))
    partial = lax.all_to_all(partial, ("sx", "sy"), 0, 0, tiled=True)
    spectral_cot = partial.astype(f32).sum(axis=0).astype(bf16)
    every_cot = jnp.broadcast_to(spectral_cot[None], (SNAPS, MODES, 2 * CO))
    every_cot = lax.all_to_all(every_cot, "dp", 0, 0, tiled=True)
    state = (2 * OWN * MODES, CO)
    weight = master.reshape(state)
    got = mix(every_cot, weight, spectrum.reshape(2 * MODES, CI))
    got = got.reshape(SNAPS * CORES, 2, 2 * OWN * MODES)
    got = lax.all_to_all(got, ("dp", "sy"), 0, 0, tiled=True, axis_index_groups=planes())
    got = got.reshape(SNAPS, CORES, 2, 2 * OWN * MODES)
    modes = lax.all_to_all(turn(got), ("sx", "sy"), 0, 0, tiled=True, axis_index_groups=columns())
    input_grad, *states = finish(
        place, modes, every_cot, got, weight, moment1.reshape(state), moment2.reshape(state)
    )
    return (input_grad.reshape(cotangent.shape), *(s.reshape(master.shape) for s in states))


def solution(mesh):
    grid = P("dp", "sx", "sy", None, None)
    state = P("dp", None, "sx", "sy", None, None)
    in_specs = (grid, P(None, "dp", "sx", "sy", None, None), state, state, state)
    out_specs = (grid, state, state, state)
    return jax.shard_map(shards, mesh=mesh, in_specs=in_specs, out_specs=out_specs, check_vma=False)
```
